256 devices in a mesh: row: 8 (over z), col: 4 (over y), depth: 8 (over x, core).
Axes of the slice: x: 4, y: 4, z: 8, core: 2. Of those that a mesh axis runs over, the one named last changes fastest.
Arguments:
- tokens: bfloat16 [768, 12288], P(('col', 'depth'), 'row'), may hold values from -6 to 6
- widen: bfloat16 [12288, 24576], P('row', ('col', 'depth')), may hold values from -0.0546875 to 0.0546875
- offsets: bfloat16 [24576], P(('col', 'depth')), may hold values from -3 to 3
- narrow: bfloat16 [24576, 12288], P(('col', 'depth'), 'row'), may hold values from -0.0390625 to 0.0390625
- shifts: bfloat16 [12288], P('row'), may hold values from -3 to 3
- cotangent: bfloat16 [768, 12288], P(('col', 'depth'), 'row'), may hold values from -4 to 4
Outputs:
- layer_out: bfloat16 [768, 12288], P(('col', 'depth'), 'row')
- token_grad: bfloat16 [768, 12288], P(('col', 'depth'), 'row')
- widen_grad: bfloat16 [12288, 24576], P('row', ('col', 'depth'))
- narrow_grad: bfloat16 [24576, 12288], P(('col', 'depth'), 'row')
- offsets_grad: float32 [24576], P(('col', 'depth'))
- shifts_grad: float32 [12288], P('row')
The draws below stay inside these ranges and needn't reach their ends.
All inputs are finite; a program needn't handle non-finite values.
Results may differ from the reference program's by a relative error of at most 0.0049.
Values may be sent and summed in bfloat16 or wider, within the bound.
No kernel may reach another device: no remote copies, remote signals or barrier semaphores. Data moves between devices by JAX's collectives and lax.ppermute only.
A program may use at most 128 MiB of HBM per device.

```python
import math
import jax
import jax.numpy as jnp
from jax import lax

D = 12288
FF = 24576
TOKENS = 768


def level_of(rng, extent, shards, low, top_value):
    gain = 1.0
    for position, blocks in shards:
        heights = jax.random.uniform(jax.random.fold_in(jax.random.fold_in(rng, 6), position), (blocks,), jnp.float32, low / len(shards), top_value / len(shards))
        gain = gain * jnp.repeat(jnp.exp(heights), extent[position] // blocks).reshape((-1,) + (1,) * (len(extent) - 1 - position))
    return gain


def noise(rng, dims, deviation, limit, pieces=(), held_as=jnp.bfloat16):
    drawn = deviation * jax.random.normal(rng, dims, jnp.float32)
    if pieces:
        drawn = drawn * level_of(rng, dims, pieces, -0.22, 0.18)
    return jnp.clip(drawn, -limit, limit).astype(held_as)


def setup_inputs(seed: int = 0) -> dict:
    seeds = jax.random.split(jax.random.key(seed), 7)
    return {
        "tokens": noise(seeds[0], (TOKENS, D), 1.0, 6.0, ((0, 32), (1, 8))),
        "widen": noise(seeds[1], (D, FF), D ** -0.5, 0.0546875, ((0, 8), (1, 32))),
        "offsets": noise(seeds[2], (FF,), 0.5, 3.0, ((0, 32),)),
        "narrow": noise(seeds[3], (FF, D), FF ** -0.5, 0.0390625, ((0, 32), (1, 8))),
        "shifts": noise(seeds[4], (D,), 0.5, 3.0, ((0, 8),)),
        "cotangent": noise(seeds[5], (TOKENS, D), 0.5, 4.0, ((0, 32), (1, 8))),
    }


cubic_coef = 0.044715
root_coef = math.sqrt(2.0 / math.pi)

def gelu_parts(hidden_pre):
    inner = root_coef * (hidden_pre + cubic_coef * hidden_pre * hidden_pre * hidden_pre)
    tangent = jnp.tanh(inner)
    value = 0.5 * hidden_pre * (1.0 + tangent)
    slope = 0.5 * (1.0 + tangent) + 0.5 * hidden_pre * (1.0 - tangent * tangent) * root_coef * (1.0 + 3.0 * cubic_coef * hidden_pre * hidden_pre)
    return (value, slope)

def reference(tokens, widen, offsets, narrow, shifts, cotangent):
    hidden_pre = jnp.dot(tokens, widen, preferred_element_type=jnp.float32) + offsets.astype(jnp.float32)
    value, slope = gelu_parts(hidden_pre)
    hidden_act = value.astype(jnp.bfloat16)
    layer_out = (jnp.dot(hidden_act, narrow, preferred_element_type=jnp.float32) + shifts.astype(jnp.float32)).astype(jnp.bfloat16)
    act_grad = jnp.dot(cotangent, narrow.T, preferred_element_type=jnp.float32)
    pre_grad = (act_grad * slope).astype(jnp.bfloat16)
    token_grad = jnp.dot(pre_grad, widen.T, preferred_element_type=jnp.float32).astype(jnp.bfloat16)
    widen_grad = jnp.dot(tokens.T, pre_grad, preferred_element_type=jnp.float32).astype(jnp.bfloat16)
    narrow_grad = jnp.dot(hidden_act.T, cotangent, preferred_element_type=jnp.float32).astype(jnp.bfloat16)
    offsets_grad = lax.optimization_barrier(jnp.sum(pre_grad.astype(jnp.float32), axis=0))
    shifts_grad = lax.optimization_barrier(jnp.sum(cotangent.astype(jnp.float32), axis=0))
    return (layer_out, token_grad, widen_grad, narrow_grad, offsets_grad, shifts_grad)
```

```python
import math

import jax
import jax.numpy as jnp
from jax import lax
from jax.sharding import PartitionSpec as P

cubic_coef = 0.044715
root_coef = math.sqrt(2.0 / math.pi)
bf16, f32 = jnp.bfloat16, jnp.float32


def gelu_parts(hidden_pre):
    inner = root_coef * (hidden_pre + cubic_coef * hidden_pre * hidden_pre * hidden_pre)
    tangent = jnp.tanh(inner)
    value = 0.5 * hidden_pre * (1.0 + tangent)
    slope = 0.5 * (1.0 + tangent) + 0.5 * hidden_pre * (1.0 - tangent * tangent) * root_coef * (
        1.0 + 3.0 * cubic_coef * hidden_pre * hidden_pre
    )
    return (value, slope)


def along_x(v, k):
    return lax.ppermute(v, "depth", [(i, (i + 2 * k) % 8) for i in range(8)])


def along_y(v, k):
    return lax.ppermute(v, "col", [(i, (i + k) % 4) for i in range(4)])


def along_z(v, k):
    return lax.ppermute(v, "row", [(i, (i + k) % 8) for i in range(8)])


def swap_cores(v):
    return lax.ppermute(v, "depth", [(i, i ^ 1) for i in range(8)])


def gather_four(v, move, far_up):
    one = move(v, -1)
    three = move(v, 1)
    two = move(one, -1) if far_up else move(three, 1)
    return [v, one, two, three]


def gather_tokens(shard, x_first):
    width = shard.shape[1]
    if x_first:
        line = jnp.concatenate(gather_four(shard, along_x, True), axis=0)
        own = jnp.concatenate(gather_four(line, along_y, True), axis=0)
    else:
        line = jnp.concatenate(gather_four(shard, along_y, True), axis=0)
        lines = [b.reshape(4, 24, width) for b in gather_four(line, along_x, True)]
        own = jnp.stack(lines, axis=1).reshape(384, width)
    return own, swap_cores(own)


def reduce_four(chunks, move, wire):
    def sent(v, k):
        return move(v.astype(wire), k).astype(f32)

    return chunks[0] + sent(chunks[1], 1) + sent(chunks[3], -1) + sent(chunks[2], 2)


def reduce_tokens(part, x_first):
    width = part.shape[1]
    other = swap_cores(part[384:].astype(bf16))
    total = (part[:384] + other.astype(f32)).reshape(4, 4, 24, width)
    if x_first:
        line = reduce_four([total[:, d].reshape(96, width) for d in range(4)], along_x, bf16)
        second = along_y
    else:
        line = reduce_four([total[d].reshape(96, width) for d in range(4)], along_y, bf16)
        second = along_x
    return reduce_four([line[24 * d : 24 * (d + 1)] for d in range(4)], second, f32)


def reduce_row(part, turn):
    place = lax.axis_index("row")
    blocks = part.reshape(8, 96, part.shape[1])

    def term(k):
        return lax.dynamic_index_in_dim(blocks, (place + turn * k + 16) % 8, 0, keepdims=False)

    near = along_z(jnp.stack([term(4).astype(bf16), term(2).astype(bf16)]), turn)
    back = along_z(term(-3).astype(bf16), -turn)
    last = along_z(term(-1).astype(bf16), -turn)
    third = along_z((near[0].astype(f32) + term(3)).astype(bf16), 3 * turn)
    first = along_z((near[1].astype(f32) + term(1)).astype(bf16), turn)
    second = along_z((back.astype(f32) + term(-2)).astype(bf16), -2 * turn)
    return term(0) + third.astype(f32) + first.astype(f32) + second.astype(f32) + last.astype(f32)


def collect_row(share, turn):
    place = lax.axis_index("row")
    whole = jnp.zeros((768, share.shape[1]), share.dtype)

    def put(whole, block, k):
        return lax.dynamic_update_slice(whole, block, ((place - k * turn + 16) % 8 * 96, 0))

    whole = put(whole, share, 0)
    ahead = behind = share
    for k in (1, 2, 3, 4):
        ahead = along_z(ahead, turn)
        whole = put(whole, ahead, k)
        if k < 4:
            behind = along_z(behind, -turn)
            whole = put(whole, behind, -k)
    return whole


def contract_last(left, right):
    return lax.dot_general(left, right, (((1,), (1,)), ((), ())), preferred_element_type=f32)


def contract_first(left, right):
    return lax.dot_general(left, right, (((0,), (0,)), ((), ())), preferred_element_type=f32)


def body(tokens, widen, offsets, narrow, shifts, cotangent):
    tok_all = jnp.concatenate(gather_tokens(tokens, True), axis=0)
    cot_all = jnp.concatenate(gather_tokens(cotangent, False), axis=0)
    pre_part = jnp.dot(tok_all, widen, preferred_element_type=f32)
    act_part = contract_last(cot_all, narrow)
    hidden_pre = reduce_row(pre_part, 1) + offsets.astype(f32)
    act_grad = reduce_row(act_part, -1)
    value, slope = gelu_parts(hidden_pre)
    act_all = collect_row(value.astype(bf16), 1)
    grad_all = collect_row((act_grad * slope).astype(bf16), -1)
    out_part = jnp.dot(act_all, narrow, preferred_element_type=f32)
    in_part = contract_last(grad_all, widen)
    layer_out = (reduce_tokens(out_part, False) + shifts.astype(f32)).astype(bf16)
    token_grad = reduce_tokens(in_part, True).astype(bf16)
    widen_grad = contract_first(tok_all, grad_all).astype(bf16)
    narrow_grad = contract_first(act_all, cot_all).astype(bf16)
    offsets_grad = jnp.sum(grad_all, axis=0, dtype=f32)
    shifts_grad = jnp.sum(cot_all, axis=0, dtype=f32)
    return (layer_out, token_grad, widen_grad, narrow_grad, offsets_grad, shifts_grad)


def solution(mesh):
    return jax.shard_map(
        body,
        mesh=mesh,
        in_specs=(
            P(("col", "depth"), "row"),
            P("row", ("col", "depth")),
            P(("col", "depth")),
            P(("col", "depth"), "row"),
            P("row"),
            P(("col", "depth"), "row"),
        ),
        out_specs=(
            P(("col", "depth"), "row"),
            P(("col", "depth"), "row"),
            P("row", ("col", "depth")),
            P(("col", "depth"), "row"),
            P(("col", "depth")),
            P("row"),
        ),
        check_vma=False,
    )
```

```python
import math

import jax
import jax.numpy as jnp
from jax import lax
from jax.sharding import PartitionSpec as P

cubic_coef = 0.044715
root_coef = math.sqrt(2.0 / math.pi)
bf16, f32 = jnp.bfloat16, jnp.float32


def gelu_parts(hidden_pre):
    inner = root_coef * (hidden_pre + cubic_coef * hidden_pre * hidden_pre * hidden_pre)
    tangent = jnp.tanh(inner)
    value = 0.5 * hidden_pre * (1.0 + tangent)
    slope = 0.5 * (1.0 + tangent) + 0.5 * hidden_pre * (1.0 - tangent * tangent) * root_coef * (
        1.0 + 3.0 * cubic_coef * hidden_pre * hidden_pre
    )
    return (value, slope)


def along_x(v, k):
    return lax.ppermute(v, "depth", [(i, (i + 2 * k) % 8) for i in range(8)])


def along_y(v, k):
    return lax.ppermute(v, "col", [(i, (i + k) % 4) for i in range(4)])


def along_z(v, k):
    return lax.ppermute(v, "row", [(i, (i + k) % 8) for i in range(8)])


def swap_cores(v):
    return lax.ppermute(v, "depth", [(i, i ^ 1) for i in range(8)])


def gather_four(v, move, direct):
    one = move(v, -1)
    three = move(v, 1)
    two = move(v, 2) if direct else move(one, -1)
    return [v, one, two, three]


def gather_tokens(shard, x_first):
    width = shard.shape[1]
    if x_first:
        line = jnp.concatenate(gather_four(shard, along_x, True), axis=0)
        own = jnp.concatenate(gather_four(line, along_y, False), axis=0)
    else:
        line = jnp.concatenate(gather_four(shard, along_y, True), axis=0)
        lines = [b.reshape(4, 24, width) for b in gather_four(line, along_x, False)]
        own = jnp.stack(lines, axis=1).reshape(384, width)
    return own, swap_cores(own)


def reduce_four(chunks, move, wire):
    def sent(v, k):
        return move(v.astype(wire), k).astype(f32)

    return chunks[0] + sent(chunks[1], 1) + sent(chunks[3], -1) + sent(chunks[2], 2)


def add_cores(part):
    other = swap_cores(part[384:].astype(bf16))
    return part[:384] + other.astype(f32)


def reduce_tokens(total, x_first):
    width = total.shape[1]
    total = total.reshape(4, 4, 24, width)
    if x_first:
        line = reduce_four([total[:, d].reshape(96, width) for d in range(4)], along_x, bf16)
        second = along_y
    else:
        line = reduce_four([total[d].reshape(96, width) for d in range(4)], along_y, bf16)
        second = along_x
    return reduce_four([line[24 * d : 24 * (d + 1)] for d in range(4)], second, f32)


def reduce_row(part, turn):
    place = lax.axis_index("row")
    blocks = part.reshape(8, 96, part.shape[1])

    def term(k):
        return lax.dynamic_index_in_dim(blocks, (place + turn * k + 16) % 8, 0, keepdims=False)

    def sent(v, k):
        return along_z(v.astype(bf16), turn * k).astype(f32)

    up = sent(term(4), 1)
    down = sent(term(-3), -1)
    near = sent(term(1), 1)
    up = sent(up + term(3), 1)
    down = sent(down + term(-2), -1)
    up = sent(up + term(2), 2)
    down = sent(down + term(-1), -1)
    return term(0) + up + down + near


def collect_row(share, turn):
    place = lax.axis_index("row")
    blocks = {0: share}
    ahead = behind = share
    for k in (1, 2, 3, 4):
        ahead = along_z(ahead, turn)
        blocks[-turn * k % 8] = ahead
        if k < 4:
            behind = along_z(behind, -turn)
            blocks[turn * k % 8] = behind
    twice = jnp.concatenate([blocks[k] for k in range(8)] * 2, axis=0)
    return lax.dynamic_slice_in_dim(twice, (8 - place) % 8 * 96, 768, 0)


def contract_last(left, right):
    return lax.dot_general(left, right, (((1,), (1,)), ((), ())), preferred_element_type=f32)


def contract_first(left, right):
    return lax.dot_general(left, right, (((0,), (0,)), ((), ())), preferred_element_type=f32)


def body(tokens, widen, offsets, narrow, shifts, cotangent):
    tok_all = jnp.concatenate(gather_tokens(tokens, True), axis=0)
    cot_all = jnp.concatenate(gather_tokens(cotangent, False), axis=0)
    pre_part = jnp.dot(tok_all, widen, preferred_element_type=f32)
    act_part = contract_last(cot_all, narrow)
    hidden_pre = reduce_row(pre_part, 1) + offsets.astype(f32)
    act_grad = reduce_row(act_part, -1)
    value, slope = gelu_parts(hidden_pre)
    act_all = collect_row(value.astype(bf16), 1)
    grad_all = collect_row((act_grad * slope).astype(bf16), -1)
    out_part = jnp.dot(act_all, narrow, preferred_element_type=f32)
    in_part = contract_last(grad_all, widen)
    out_chip, in_chip = add_cores(out_part), add_cores(in_part)
    act_late, grad_late, out_chip, in_chip = lax.optimization_barrier(
        (act_all, grad_all, out_chip, in_chip)
    )
    layer_out = (reduce_tokens(out_chip, False) + shifts.astype(f32)).astype(bf16)
    token_grad = reduce_tokens(in_chip, True).astype(bf16)
    widen_grad = contract_first(tok_all, grad_late).astype(bf16)
    narrow_grad = contract_first(act_late, cot_all).astype(bf16)
    offsets_grad = jnp.sum(grad_late, axis=0, dtype=f32)
    shifts_grad = jnp.sum(cot_all, axis=0, dtype=f32)
    return (layer_out, token_grad, widen_grad, narrow_grad, offsets_grad, shifts_grad)


def solution(mesh):
    return jax.shard_map(
        body,
        mesh=mesh,
        in_specs=(
            P(("col", "depth"), "row"),
            P("row", ("col", "depth")),
            P(("col", "depth")),
            P(("col", "depth"), "row"),
            P("row"),
            P(("col", "depth"), "row"),
        ),
        out_specs=(
            P(("col", "depth"), "row"),
            P(("col", "depth"), "row"),
            P("row", ("col", "depth")),
            P(("col", "depth"), "row"),
            P(("col", "depth")),
            P("row"),
        ),
        check_vma=False,
    )
```

```python
import functools
import math

import jax
import jax.numpy as jnp
from jax import lax
from jax.experimental import pallas as pl
from jax.experimental.pallas import tpu as pltpu
from jax.sharding import PartitionSpec as P

cubic_coef = 0.044715
root_coef = math.sqrt(2.0 / math.pi)
bf16, f32 = jnp.bfloat16, jnp.float32


def gelu_parts(hidden_pre):
    inner = root_coef * (hidden_pre + cubic_coef * hidden_pre * hidden_pre * hidden_pre)
    tangent = jnp.tanh(inner)
    value = 0.5 * hidden_pre * (1.0 + tangent)
    slope = 0.5 * (1.0 + tangent) + 0.5 * hidden_pre * (1.0 - tangent * tangent) * root_coef * (
        1.0 + 3.0 * cubic_coef * hidden_pre * hidden_pre
    )
    return (value, slope)


def along_x(v, k):
    return lax.ppermute(v, "depth", [(i, (i + 2 * k) % 8) for i in range(8)])


def along_y(v, k):
    return lax.ppermute(v, "col", [(i, (i + k) % 4) for i in range(4)])


def along_z(v, k):
    return lax.ppermute(v, "row", [(i, (i + k) % 8) for i in range(8)])


def swap_cores(v):
    return lax.ppermute(v, "depth", [(i, i ^ 1) for i in range(8)])


def whole(shape):
    return pl.BlockSpec(shape, lambda *_: (0,) * len(shape))


def params():
    return pltpu.CompilerParams(vmem_limit_bytes=32 * 1024 * 1024)


def stack_kernel(axis, *refs):
    out = refs[4]
    for d in range(4):
        if axis == 0:
            out[d] = refs[d][...]
        else:
            for n in range(out.shape[0]):
                out[n, d] = refs[d][n]


def stack_four(blocks, axis):
    n, rows, width = blocks[0].shape
    shape = (4, n, rows, width) if axis == 0 else (n, 4, rows, width)
    return pl.pallas_call(
        functools.partial(stack_kernel, axis),
        out_shape=jax.ShapeDtypeStruct(shape, bf16),
        in_specs=[whole((n, rows, width))] * 4,
        out_specs=whole(shape),
        grid=(1,),
        compiler_params=params(),
        cost_estimate=pl.CostEstimate(
            flops=0, bytes_accessed=16 * n * rows * width, transcendentals=0
        ),
    )(*blocks)


def gather_four(v, move, direct):
    one = move(v, -1)
    three = move(v, 1)
    two = move(v, 2) if direct else move(one, -1)
    return [v, one, two, three]


def gather_tokens(shard, x_first):
    width = shard.shape[1]
    first, second = (along_x, along_y) if x_first else (along_y, along_x)
    line = stack_four(gather_four(shard[None], first, True), 0).reshape(4, 24, width)
    own = stack_four(gather_four(line, second, False), 0 if x_first else 1).reshape(384, width)
    return own, swap_cores(own)


def product(left, right, flip):
    return lax.dot_general(
        left, right, (((1,), (1 if flip else 0,)), ((), ())), preferred_element_type=f32
    )


def column_sums(rows):
    return jnp.dot(jnp.ones((8, rows.shape[0]), bf16), rows, preferred_element_type=f32)


def into_hidden_kernel(flip, own, other, weight, part, rows, sums):
    @pl.when(pl.program_id(0) == 0)
    def _():
        rows[0:384, :] = own[...]
        rows[384:768, :] = other[...]
        sums[...] = column_sums(rows[...])

    part[...] = product(rows[...], weight[...], flip)


def into_hidden(own, other, weight, flip):
    k = own.shape[1]
    n = weight.shape[0] if flip else weight.shape[1]
    step = 256
    weight_spec = (
        pl.BlockSpec((step, k), lambda j: (j, 0)) if flip else pl.BlockSpec((k, step), lambda j: (0, j))
    )
    return pl.pallas_call(
        functools.partial(into_hidden_kernel, flip),
        out_shape=(
            jax.ShapeDtypeStruct((768, n), f32),
            jax.ShapeDtypeStruct((768, k), bf16),
            jax.ShapeDtypeStruct((8, k), f32),
        ),
        grid=(n // step,),
        in_specs=[whole((384, k)), whole((384, k)), weight_spec],
        out_specs=(pl.BlockSpec((768, step), lambda j: (0, j)), whole((768, k)), whole((8, k))),
        compiler_params=params(),
        cost_estimate=pl.CostEstimate(
            flops=2 * 768 * n * k, bytes_accessed=4 * 768 * n + 4 * 768 * k + 2 * n * k, transcendentals=0
        ),
    )(own, other, weight)


def out_of_hidden_kernel(flip, place, *refs):
    blocks, weight = refs[:8], refs[8]
    keep, send, rows, sums = refs[9:]

    @pl.when(pl.program_id(0) == 0)
    def _():
        for k in range(8):
            first = pl.multiple_of(lax.rem(place[0] + k, 8) * 96, 96)
            rows[pl.ds(first, 96), :] = blocks[k][...]
        sums[...] = column_sums(rows[...])

    part = product(rows[...], weight[...], flip)
    keep[...] = part[:384]
    send[...] = part[384:].astype(bf16)


def out_of_hidden(blocks, weight, flip):
    k = blocks[0].shape[1]
    n = weight.shape[0] if flip else weight.shape[1]
    step = 512
    weight_spec = (
        pl.BlockSpec((step, k), lambda j: (j, 0)) if flip else pl.BlockSpec((k, step), lambda j: (0, j))
    )
    half = pl.BlockSpec((384, step), lambda j: (0, j))
    return pl.pallas_call(
        functools.partial(out_of_hidden_kernel, flip),
        out_shape=(
            jax.ShapeDtypeStruct((384, n), f32),
            jax.ShapeDtypeStruct((384, n), bf16),
            jax.ShapeDtypeStruct((768, k), bf16),
            jax.ShapeDtypeStruct((8, k), f32),
        ),
        grid=(n // step,),
        in_specs=[pl.BlockSpec(memory_space=pltpu.SMEM)] + [whole((96, k))] * 8 + [weight_spec],
        out_specs=(half, half, whole((768, k)), whole((8, k))),
        compiler_params=params(),
        cost_estimate=pl.CostEstimate(
            flops=2 * 768 * n * k, bytes_accessed=6 * 384 * n + 4 * 768 * k + 2 * n * k, transcendentals=0
        ),
    )(lax.axis_index("row").astype(jnp.int32).reshape(1), *blocks, weight)


def reduce_four(chunks, move, wire):
    def sent(v, k):
        return move(v.astype(wire), k).astype(f32)

    return chunks[0] + sent(chunks[1], 1) + sent(chunks[3], -1) + sent(chunks[2], 2)


def add_cores(keep, send):
    return keep + swap_cores(send).astype(f32)


def reduce_tokens(total, x_first):
    width = total.shape[1]
    total = total.reshape(4, 4, 24, width)
    if x_first:
        line = reduce_four([total[:, d].reshape(96, width) for d in range(4)], along_x, bf16)
        second = along_y
    else:
        line = reduce_four([total[d].reshape(96, width) for d in range(4)], along_y, bf16)
        second = along_x
    return reduce_four([line[24 * d : 24 * (d + 1)] for d in range(4)], second, f32)


def reduce_row(part, turn):
    place = lax.axis_index("row")
    blocks = part.reshape(8, 96, part.shape[1])

    def term(k):
        return lax.dynamic_index_in_dim(blocks, (place + turn * k + 16) % 8, 0, keepdims=False)

    def sent(v, k):
        return along_z(v.astype(bf16), turn * k).astype(f32)

    near = along_z(jnp.stack([term(4).astype(bf16), term(2).astype(bf16)]), turn)
    back = sent(term(-3), -1)
    last = sent(term(-1), -1)
    third = sent(near[0].astype(f32) + term(3), 3)
    first = sent(near[1].astype(f32) + term(1), 1)
    second = sent(back + term(-2), -2)
    return term(0) + third + first + second + last


def collect_row(share, turn):
    blocks = {0: share}
    ahead = behind = share
    for k in (1, 2, 3, 4):
        ahead = along_z(ahead, turn)
        blocks[-turn * k % 8] = ahead
        if k < 4:
            behind = along_z(behind, -turn)
            blocks[turn * k % 8] = behind
    return [blocks[k] for k in range(8)]


def contract_first(left, right):
    return lax.dot_general(left, right, (((0,), (0,)), ((), ())), preferred_element_type=f32)


def body(tokens, widen, offsets, narrow, shifts, cotangent):
    pre_part, tok_all, _ = into_hidden(*gather_tokens(tokens, True), widen, False)
    act_part, cot_all, cot_sums = into_hidden(*gather_tokens(cotangent, False), narrow, True)
    hidden_pre = reduce_row(pre_part, 1) + offsets.astype(f32)
    act_grad = reduce_row(act_part, -1)
    value, slope = gelu_parts(hidden_pre)
    act_blocks = collect_row(value.astype(bf16), 1)
    grad_blocks = collect_row((act_grad * slope).astype(bf16), -1)
    out_keep, out_send, act_all, _ = out_of_hidden(act_blocks, narrow, False)
    in_keep, in_send, grad_all, grad_sums = out_of_hidden(grad_blocks, widen, True)
    out_chip, in_chip = add_cores(out_keep, out_send), add_cores(in_keep, in_send)
    act_late, grad_late, out_chip, in_chip = lax.optimization_barrier(
        (act_all, grad_all, out_chip, in_chip)
    )
    layer_out = (reduce_tokens(out_chip, False) + shifts.astype(f32)).astype(bf16)
    token_grad = reduce_tokens(in_chip, True).astype(bf16)
    widen_grad = contract_first(tok_all, grad_late).astype(bf16)
    narrow_grad = contract_first(act_late, cot_all).astype(bf16)
    return (layer_out, token_grad, widen_grad, narrow_grad, grad_sums[0], cot_sums[0])


def solution(mesh):
    return jax.shard_map(
        body,
        mesh=mesh,
        in_specs=(
            P(("col", "depth"), "row"),
            P("row", ("col", "depth")),
            P(("col", "depth")),
            P(("col", "depth"), "row"),
            P("row"),
            P(("col", "depth"), "row"),
        ),
        out_specs=(
            P(("col", "depth"), "row"),
            P(("col", "depth"), "row"),
            P("row", ("col", "depth")),
            P(("col", "depth"), "row"),
            P(("col", "depth")),
            P("row"),
        ),
        check_vma=False,
    )
```

```python
import functools
import math

import jax
import jax.numpy as jnp
from jax import lax
from jax.experimental import pallas as pl
from jax.experimental.pallas import tpu as pltpu
from jax.sharding import PartitionSpec as P

cubic_coef = 0.044715
root_coef = math.sqrt(2.0 / math.pi)
bf16, f32 = jnp.bfloat16, jnp.float32


def gelu_parts(hidden_pre):
    inner = root_coef * (hidden_pre + cubic_coef * hidden_pre * hidden_pre * hidden_pre)
    tangent = jnp.tanh(inner)
    value = 0.5 * hidden_pre * (1.0 + tangent)
    slope = 0.5 * (1.0 + tangent) + 0.5 * hidden_pre * (1.0 - tangent * tangent) * root_coef * (
        1.0 + 3.0 * cubic_coef * hidden_pre * hidden_pre
    )
    return (value, slope)


def along_x(v, k):
    return lax.ppermute(v, "depth", [(i, (i + 2 * k) % 8) for i in range(8)])


def along_y(v, k):
    return lax.ppermute(v, "col", [(i, (i + k) % 4) for i in range(4)])


def along_z(v, k):
    return lax.ppermute(v, "row", [(i, (i + k) % 8) for i in range(8)])


def swap_cores(v):
    return lax.ppermute(v, "depth", [(i, i ^ 1) for i in range(8)])


def whole(shape):
    return pl.BlockSpec(shape, lambda *_: (0,) * len(shape))


def columns(shape):
    return pl.BlockSpec(shape, lambda j: (0,) * (len(shape) - 1) + (j,))


def call(kernel, grid, ins, in_specs, outs, out_specs, flops=0, scratch=()):
    moved = sum(math.prod(a.shape) * a.dtype.itemsize for a in (*ins, *outs))
    return pl.pallas_call(
        kernel,
        out_shape=tuple(outs),
        grid=(grid,),
        in_specs=in_specs,
        out_specs=tuple(out_specs),
        scratch_shapes=scratch,
        compiler_params=pltpu.CompilerParams(vmem_limit_bytes=48 * 1024 * 1024),
        cost_estimate=pl.CostEstimate(flops=flops, bytes_accessed=moved, transcendentals=0),
    )(*ins)


def like(shape, dtype):
    return jax.ShapeDtypeStruct(shape, dtype)


def stack_kernel(inner, *refs):
    fore, back, fore_out, back_out = refs[0:4], refs[4:8], refs[8], refs[9]
    for d in range(4):
        fore_out[d] = fore[d][...]
        if inner:
            for n in range(4):
                back_out[n, d] = back[d][n]
        else:
            back_out[d] = back[d][...]


def stack_lines(fore, back):
    shape = fore[0].shape
    out = (4, *shape)
    return call(
        functools.partial(stack_kernel, False), 1, (*fore, *back), [whole(shape)] * 8, [like(out, bf16)] * 2, [whole(out)] * 2
    )


def stack_planes(fore, back):
    shape = fore[0].shape
    out = (4, *shape)
    return call(
        functools.partial(stack_kernel, True), 1, (*fore, *back), [whole(shape)] * 8, [like(out, bf16)] * 2, [whole(out)] * 2
    )


def product(left, right, flip):
    return lax.dot_general(
        left, right, (((1,), (1 if flip else 0,)), ((), ())), preferred_element_type=f32
    )


def column_sums(rows):
    return jnp.dot(jnp.ones((8, rows.shape[0]), bf16), rows, preferred_element_type=f32)


SENT, KEPT = (4, -3, 1), (0, 3, 2, -2, -1)


def into_hidden_kernel(turn, flip, place, own, other, weight, *outs):
    terms, (rows, sums, part) = outs[:8], outs[8:]
    step = rows.shape[1]
    here = pl.ds(pl.multiple_of(pl.program_id(0) * step, step), step)
    rows[0:384, :] = own[:, here]
    rows[384:768, :] = other[:, here]
    sums[...] = column_sums(rows[...])
    part[0:384, :] = product(own[...], weight[...], flip)
    part[384:768, :] = product(other[...], weight[...], flip)

    def term(k):
        first = pl.multiple_of(lax.rem(place[0] + turn * k + 16, 8) * 96, 96)
        return part[pl.ds(first, 96), :]

    for out, k in zip(terms, SENT + KEPT):
        out[...] = term(k).astype(out.dtype)


def into_hidden(place, own, other, weight, turn, flip):
    k = own.shape[1]
    n = weight.shape[0] if flip else weight.shape[1]
    steps = 3
    step, wide = n // steps, k // steps
    half = whole((384, k))
    weight_spec = pl.BlockSpec((step, k), lambda j: (j, 0)) if flip else columns((k, step))
    got = call(
        functools.partial(into_hidden_kernel, turn, flip),
        steps,
        (place, own, other, weight),
        [pl.BlockSpec(memory_space=pltpu.SMEM), half, half, weight_spec],
        [like((96, n), bf16)] * 3 + [like((96, n), f32)] * 5 + [like((768, k), bf16), like((8, k), f32)],
        [columns((96, step))] * 8 + [columns((768, wide)), columns((8, wide))],
        flops=2 * 768 * n * k,
        scratch=[pltpu.VMEM((768, step), f32)],
    )
    return dict(zip(SENT + KEPT, got[:8])), *got[8:]


def out_of_hidden_kernel(flip, place, *refs):
    blocks, weight, (keep, send, rows, sums) = refs[:8], refs[8], refs[9:]

    @pl.when(pl.program_id(0) == 0)
    def _():
        for k in range(8):
            first = pl.multiple_of(lax.rem(place[0] + k, 8) * 96, 96)
            rows[pl.ds(first, 96), :] = blocks[k][...]
        sums[...] = column_sums(rows[...])

    part = product(rows[...], weight[...], flip)
    keep[...] = part[:384]
    send[...] = part[384:].astype(bf16)


def out_of_hidden(place, blocks, weight, flip):
    k = blocks[0].shape[1]
    n = weight.shape[0] if flip else weight.shape[1]
    step = 512
    half, rows = columns((384, step)), whole((768, k))
    weight_spec = pl.BlockSpec((step, k), lambda j: (j, 0)) if flip else columns((k, step))
    return call(
        functools.partial(out_of_hidden_kernel, flip),
        n // step,
        (place, *blocks, weight),
        [pl.BlockSpec(memory_space=pltpu.SMEM)] + [whole((96, k))] * 8 + [weight_spec],
        [like((384, n), f32), like((384, n), bf16), like((768, k), bf16), like((8, k), f32)],
        [half, half, rows, whole((8, k))],
        flops=2 * 768 * n * k,
    )


def chip_kernel(by_x, keep, got, *outs):
    for d in range(4):
        if by_x:
            total = keep[:, d] + got[:, d].astype(f32)
        else:
            total = keep[d] + got[d].astype(f32)
        outs[d][...] = total.astype(outs[d].dtype)


def chip_sums(keep, got, by_x):
    n = keep.shape[1]
    step = 512
    return call(
        functools.partial(chip_kernel, by_x),
        n // step,
        [v.reshape(4, 4, 24, n) for v in (keep, got)],
        [columns((4, 4, 24, step))] * 2,
        [like((4, 24, n), f32)] + [like((4, 24, n), bf16)] * 3,
        [columns((4, 24, step))] * 4,
    )


def line_kernel(*refs):
    for ins, outs in ((refs[0:4], refs[8:12]), (refs[4:8], refs[12:16])):
        for d in range(4):
            total = ins[0][d]
            for v in ins[1:]:
                total += v[d].astype(f32)
            outs[d][...] = total.astype(outs[d].dtype)


def line_sums(fore, back):
    n = fore[0].shape[2]
    outs = [like((24, n), bf16 if d == 2 else f32) for d in range(4)]
    return call(
        line_kernel, 1, (*fore, *back), [whole((4, 24, n))] * 8, outs * 2, [whole((24, n))] * 8
    )


def gather_four(v, move, direct):
    one = move(v, -1)
    three = move(v, 1)
    two = move(v, 2) if direct else move(one, -1)
    return [v, one, two, three]


def gather_both(fore, back):
    width = fore.shape[1]
    fore, back = stack_lines(gather_four(fore, along_x, True), gather_four(back, along_y, True))
    fore, back = stack_planes(gather_four(fore, along_y, False), gather_four(back, along_x, False))
    return fore.reshape(384, width), back.reshape(384, width)


def collect_row(share, turn):
    blocks = {0: share}
    ahead = behind = share
    for k in (1, 2, 3, 4):
        ahead = along_z(ahead, turn)
        blocks[-turn * k % 8] = ahead
        if k < 4:
            behind = along_z(behind, -turn)
            blocks[turn * k % 8] = behind
    return [blocks[k] for k in range(8)]


def reduce_row(terms, turn):
    def sent(v, k):
        return along_z(v.astype(bf16), turn * k).astype(f32)

    up, down, near = sent(terms[4], 1), sent(terms[-3], -1), sent(terms[1], 1)
    up, down = sent(up + terms[3], 1), sent(down + terms[-2], -1)
    up, down = sent(up + terms[2], 2), sent(down + terms[-1], -1)
    return terms[0] + up + down + near


def scatter_four(pieces, move):
    return [pieces[0], move(pieces[2], 2), move(pieces[1], 1), move(pieces[3], -1)]


def scatter_last(pieces, move):
    return sum(v.astype(f32) for v in scatter_four(pieces, move))


def contract_first(left, right):
    return lax.dot_general(left, right, (((0,), (0,)), ((), ())), preferred_element_type=f32)


def body(tokens, widen, offsets, narrow, shifts, cotangent):
    place = lax.axis_index("row").astype(jnp.int32).reshape(1)
    tok_own, cot_own = gather_both(tokens, cotangent)
    fore, tok_all, _ = into_hidden(place, tok_own, swap_cores(tok_own), widen, 1, False)
    back, cot_all, cot_sums = into_hidden(place, cot_own, swap_cores(cot_own), narrow, -1, True)
    value, slope = gelu_parts(reduce_row(fore, 1) + offsets.astype(f32))
    act_grad = reduce_row(back, -1)
    act_blocks = collect_row(value.astype(bf16), 1)
    grad_blocks = collect_row((act_grad * slope).astype(bf16), -1)
    act_blocks, grad_blocks = lax.optimization_barrier((act_blocks, grad_blocks))
    f_keep, f_send, act_all, _ = out_of_hidden(place, act_blocks, narrow, False)
    b_keep, b_send, grad_all, grad_sums = out_of_hidden(place, grad_blocks, widen, True)
    f_got, b_got = swap_cores(f_send), swap_cores(b_send)
    fore, back = chip_sums(f_keep, f_got, False), chip_sums(b_keep, b_got, True)
    act_late, grad_late, *pieces = lax.optimization_barrier((act_all, grad_all, *fore, *back))
    fore, back = scatter_four(pieces[:4], along_y), scatter_four(pieces[4:], along_x)
    narrow_grad = contract_first(act_late, cot_all).astype(bf16)
    widen_grad = contract_first(tok_all, grad_late).astype(bf16)
    offsets_grad, shifts_grad = grad_sums[0], cot_sums[0]
    narrow_grad, widen_grad, offsets_grad, shifts_grad, fore, back = lax.optimization_barrier(
        (narrow_grad, widen_grad, offsets_grad, shifts_grad, fore, back)
    )
    lines = line_sums(fore, back)
    layer_out = (scatter_last(lines[:4], along_x) + shifts.astype(f32)).astype(bf16)
    token_grad = scatter_last(lines[4:], along_y).astype(bf16)
    return (layer_out, token_grad, widen_grad, narrow_grad, offsets_grad, shifts_grad)


def solution(mesh):
    return jax.shard_map(
        body,
        mesh=mesh,
        in_specs=(
            P(("col", "depth"), "row"),
            P("row", ("col", "depth")),
            P(("col", "depth")),
            P(("col", "depth"), "row"),
            P("row"),
            P(("col", "depth"), "row"),
        ),
        out_specs=(
            P(("col", "depth"), "row"),
            P(("col", "depth"), "row"),
            P("row", ("col", "depth")),
            P(("col", "depth"), "row"),
            P(("col", "depth")),
            P("row"),
        ),
        check_vma=False,
    )
```

```python
import functools
import math

import jax
import jax.numpy as jnp
from jax import lax
from jax.experimental import pallas as pl
from jax.experimental.pallas import tpu as pltpu
from jax.sharding import PartitionSpec as P

cubic_coef = 0.044715
root_coef = math.sqrt(2.0 / math.pi)
bf16, f32 = jnp.bfloat16, jnp.float32


def gelu_parts(hidden_pre):
    inner = root_coef * (hidden_pre + cubic_coef * hidden_pre * hidden_pre * hidden_pre)
    tangent = jnp.tanh(inner)
    value = 0.5 * hidden_pre * (1.0 + tangent)
    slope = 0.5 * (1.0 + tangent) + 0.5 * hidden_pre * (1.0 - tangent * tangent) * root_coef * (
        1.0 + 3.0 * cubic_coef * hidden_pre * hidden_pre
    )
    return (value, slope)


def along_x(v, k):
    return lax.ppermute(v, "depth", [(i, (i + 2 * k) % 8) for i in range(8)])


def along_y(v, k):
    return lax.ppermute(v, "col", [(i, (i + k) % 4) for i in range(4)])


def along_z(v, k):
    return lax.ppermute(v, "row", [(i, (i + k) % 8) for i in range(8)])


def swap_cores(v):
    return lax.ppermute(v, "depth", [(i, i ^ 1) for i in range(8)])


VMEM_LIMIT = 8 * 1024 * 1024


def call(kernel, ins, outs, flops=0, scratch=()):
    moved = sum(math.prod(a.shape) * a.dtype.itemsize for a in (*ins, *outs))

    def space(a):
        return pl.BlockSpec(memory_space=pltpu.SMEM if a.shape == (1,) else pltpu.VMEM)

    return pl.pallas_call(
        kernel,
        out_shape=tuple(outs),
        in_specs=[space(a) for a in ins],
        out_specs=tuple(space(a) for a in outs),
        scratch_shapes=scratch,
        compiler_params=pltpu.CompilerParams(vmem_limit_bytes=VMEM_LIMIT),
        cost_estimate=pl.CostEstimate(flops=flops, bytes_accessed=moved, transcendentals=0),
    )(*ins)


def like(shape, dtype):
    return jax.ShapeDtypeStruct(shape, dtype)


def stack_kernel(inner, *refs):
    fore, back, fore_out, back_out = refs[0:4], refs[4:8], refs[8], refs[9]
    for d in range(4):
        fore_out[d] = fore[d][...]
        if inner:
            for n in range(4):
                back_out[n, d] = back[d][n]
        else:
            back_out[d] = back[d][...]


def stack_lines(fore, back):
    out = like((4, *fore[0].shape), bf16)
    return call(functools.partial(stack_kernel, False), (*fore, *back), [out, out])


def stack_planes(fore, back):
    out = like((4, *fore[0].shape), bf16)
    return call(functools.partial(stack_kernel, True), (*fore, *back), [out, out])


def product(left, right, flip):
    return lax.dot_general(
        left, right, (((1,), (1 if flip else 0,)), ((), ())), preferred_element_type=f32
    )


def column_kernel(first, second, *outs):
    for rows, out in zip((first, second), outs):

        def add(i, total):
            return total + rows[pl.ds(pl.multiple_of(i * 16, 16), 16), :].astype(f32)

        total = lax.fori_loop(0, rows.shape[0] // 16, add, jnp.zeros((16, rows.shape[1]), f32), unroll=4)
        out[...] = jnp.sum(total, axis=0, keepdims=out.ndim == 2)


def column_sums(first, second):
    return call(column_kernel, (first, second), [like((v.shape[1],), f32) for v in (first, second)])


SENT, KEPT = (4, -3, 1), (0, 3, 2, -2, -1)


def into_hidden_kernel(turn, flip, place, own, other, weight, *outs):
    terms, rows, part = outs[:8], outs[8], outs[-1]
    step = part.shape[1]
    rows[0:384, :] = own[...]
    rows[384:768, :] = other[...]

    @pl.loop(0, terms[0].shape[1] // step)
    def _(j):
        here = pl.ds(pl.multiple_of(j * step, step), step)
        part[...] = product(rows[...], weight[here, :] if flip else weight[:, here], flip)
        for out, k in zip(terms, SENT + KEPT):
            first = pl.multiple_of(lax.rem(place[0] + turn * k + 16, 8) * 96, 96)
            out[:, here] = part[pl.ds(first, 96), :].astype(out.dtype)


def into_hidden(place, own, other, weight, turn, flip):
    k = own.shape[1]
    n = weight.shape[0] if flip else weight.shape[1]
    got = call(
        functools.partial(into_hidden_kernel, turn, flip),
        (place, own, other, weight),
        [like((96, n), bf16)] * 3 + [like((96, n), f32)] * 5 + [like((768, k), bf16)],
        flops=2 * 768 * n * k,
        scratch=[pltpu.VMEM((768, 256), f32)],
    )
    return dict(zip(SENT + KEPT, got[:8])), *got[8:]


def out_of_hidden_kernel(flip, place, *refs):
    blocks, weight, (keep, send, rows) = refs[:8], refs[8], refs[9:]
    for k in range(8):
        first = pl.multiple_of(lax.rem(place[0] + k, 8) * 96, 96)
        rows[pl.ds(first, 96), :] = blocks[k][...]
    step = 256

    @pl.loop(0, keep.shape[1] // step)
    def _(j):
        here = pl.ds(pl.multiple_of(j * step, step), step)
        part = product(rows[...], weight[here, :] if flip else weight[:, here], flip)
        keep[:, here] = part[:384]
        send[:, here] = part[384:].astype(bf16)


def out_of_hidden(place, blocks, weight, flip):
    k = blocks[0].shape[1]
    n = weight.shape[0] if flip else weight.shape[1]
    return call(
        functools.partial(out_of_hidden_kernel, flip),
        (place, *blocks, weight),
        [like((384, n), f32), like((384, n), bf16), like((768, k), bf16)],
        flops=2 * 768 * n * k,
    )


def chip_kernel(by_x, keep, got, *outs):
    for d in range(4):
        if by_x:
            total = keep[:, d] + got[:, d].astype(f32)
        else:
            total = keep[d] + got[d].astype(f32)
        outs[d][...] = total.astype(outs[d].dtype)


def chip_sums(keep, got, by_x):
    n = keep.shape[1]
    return call(
        functools.partial(chip_kernel, by_x),
        [v.reshape(4, 4, 24, n) for v in (keep, got)],
        [like((4, 24, n), f32)] + [like((4, 24, n), bf16)] * 3,
    )


def line_kernel(*refs):
    for ins, outs in ((refs[0:4], refs[8:12]), (refs[4:8], refs[12:16])):
        for d in range(4):
            total = ins[0][d]
            for v in ins[1:]:
                total += v[d].astype(f32)
            outs[d][...] = total.astype(outs[d].dtype)


def line_sums(fore, back):
    n = fore[0].shape[2]
    f_types, b_types = (f32, bf16, bf16, bf16), (f32, f32, bf16, f32)
    return call(line_kernel, (*fore, *back), [like((24, n), t) for t in f_types + b_types])


def gather_four(v, move, direct):
    one = move(v, -1)
    three = move(v, 1)
    two = move(v, 2) if direct else move(one, -1)
    return [v, one, two, three]


def gather_both(fore, back):
    width = fore.shape[1]
    fore, back = stack_lines(gather_four(fore, along_x, True), gather_four(back, along_y, True))
    fore, back = stack_planes(gather_four(fore, along_y, False), gather_four(back, along_x, False))
    return fore.reshape(384, width), back.reshape(384, width)


def collect_row(share, turn):
    blocks = {0: share}
    ahead = behind = share
    for k in (1, 2, 3, 4):
        ahead = along_z(ahead, turn)
        blocks[-turn * k % 8] = ahead
        if k < 4:
            behind = along_z(behind, -turn)
            blocks[turn * k % 8] = behind
    return [blocks[k] for k in range(8)]


def reduce_row(terms, turn):
    def sent(v, k):
        return along_z(v.astype(bf16), turn * k).astype(f32)

    up, down, near = sent(terms[4], 1), sent(terms[-3], -1), sent(terms[1], 1)
    up, down = sent(up + terms[3], 1), sent(down + terms[-2], -1)
    up, down = sent(up + terms[2], 2), sent(down + terms[-1], -1)
    return terms[0] + up + down + near


def scatter_four(pieces, move):
    return [pieces[0], move(pieces[2], 2), move(pieces[1], 1), move(pieces[3], -1)]


def contract_first(left, right):
    return lax.dot_general(left, right, (((0,), (0,)), ((), ())), preferred_element_type=f32)


def body(tokens, widen, offsets, narrow, shifts, cotangent):
    place = lax.axis_index("row").astype(jnp.int32).reshape(1)
    tok_own, cot_own = gather_both(tokens, cotangent)
    fore, tok_all = into_hidden(place, tok_own, swap_cores(tok_own), widen, 1, False)
    back, cot_all = into_hidden(place, cot_own, swap_cores(cot_own), narrow, -1, True)
    value, slope = gelu_parts(reduce_row(fore, 1) + offsets.astype(f32))
    act_grad = reduce_row(back, -1)
    act_blocks = collect_row(value.astype(bf16), 1)
    grad_blocks = collect_row((act_grad * slope).astype(bf16), -1)
    act_blocks, grad_blocks = lax.optimization_barrier((act_blocks, grad_blocks))
    f_keep, f_send, act_all = out_of_hidden(place, act_blocks, narrow, False)
    b_keep, b_send, grad_all = out_of_hidden(place, grad_blocks, widen, True)
    f_got, b_got = swap_cores(f_send), swap_cores(b_send)
    fore, back = chip_sums(f_keep, f_got, False), chip_sums(b_keep, b_got, True)
    grad_late, *pieces = lax.optimization_barrier((grad_all, *fore, *back))
    fore, back = scatter_four(pieces[:4], along_y), scatter_four(pieces[4:], along_x)
    grad_late, fore[1] = lax.optimization_barrier((grad_late, fore[1]))
    widen_grad = contract_first(tok_all, grad_late).astype(bf16)
    widen_grad, fore, back = lax.optimization_barrier((widen_grad, fore, back))
    lines = line_sums(fore, back)
    fore, back = scatter_four(lines[:4], along_x), scatter_four(lines[4:], along_y)
    act_late, grad_late, fore[1] = lax.optimization_barrier((act_all, grad_all, fore[1]))
    narrow_grad = contract_first(act_late, cot_all).astype(bf16)
    offsets_grad, shifts_grad = column_sums(grad_late, cot_all)
    layer_out = (sum(v.astype(f32) for v in fore) + shifts.astype(f32)).astype(bf16)
    token_grad = sum(v.astype(f32) for v in back).astype(bf16)
    return (layer_out, token_grad, widen_grad, narrow_grad, offsets_grad, shifts_grad)


def solution(mesh):
    return jax.shard_map(
        body,
        mesh=mesh,
        in_specs=(
            P(("col", "depth"), "row"),
            P("row", ("col", "depth")),
            P(("col", "depth")),
            P(("col", "depth"), "row"),
            P("row"),
            P(("col", "depth"), "row"),
        ),
        out_specs=(
            P(("col", "depth"), "row"),
            P(("col", "depth"), "row"),
            P("row", ("col", "depth")),
            P(("col", "depth"), "row"),
            P(("col", "depth")),
            P("row"),
        ),
        check_vma=False,
    )
```

```python
import functools
import math

import jax
import jax.numpy as jnp
from jax import lax
from jax.experimental import pallas as pl
from jax.experimental.pallas import tpu as pltpu
from jax.sharding import PartitionSpec as P

cubic_coef = 0.044715
root_coef = math.sqrt(2.0 / math.pi)
bf16, f32 = jnp.bfloat16, jnp.float32


def gelu_parts(hidden_pre):
    inner = root_coef * (hidden_pre + cubic_coef * hidden_pre * hidden_pre * hidden_pre)
    tangent = jnp.tanh(inner)
    value = 0.5 * hidden_pre * (1.0 + tangent)
    slope = 0.5 * (1.0 + tangent) + 0.5 * hidden_pre * (1.0 - tangent * tangent) * root_coef * (
        1.0 + 3.0 * cubic_coef * hidden_pre * hidden_pre
    )
    return (value, slope)


def along_x(v, k):
    return lax.ppermute(v, "depth", [(i, (i + 2 * k) % 8) for i in range(8)])


def along_y(v, k):
    return lax.ppermute(v, "col", [(i, (i + k) % 4) for i in range(4)])


def along_z(v, k):
    return lax.ppermute(v, "row", [(i, (i + k) % 8) for i in range(8)])


def swap_cores(v):
    return lax.ppermute(v, "depth", [(i, i ^ 1) for i in range(8)])


VMEM_LIMIT = 8 * 1024 * 1024


def call(kernel, ins, outs, flops=0, scratch=()):
    moved = sum(math.prod(a.shape) * a.dtype.itemsize for a in (*ins, *outs))

    def space(a):
        return pl.BlockSpec(memory_space=pltpu.SMEM if a.shape == (1,) else pltpu.VMEM)

    return pl.pallas_call(
        kernel,
        out_shape=tuple(outs),
        in_specs=[space(a) for a in ins],
        out_specs=tuple(space(a) for a in outs),
        scratch_shapes=scratch,
        compiler_params=pltpu.CompilerParams(vmem_limit_bytes=VMEM_LIMIT),
        cost_estimate=pl.CostEstimate(flops=flops, bytes_accessed=moved, transcendentals=0),
    )(*ins)


def like(shape, dtype):
    return jax.ShapeDtypeStruct(shape, dtype)


def stack_kernel(inner, *refs):
    fore, back, fore_out, back_out = refs[0:4], refs[4:8], refs[8], refs[9]
    for d in range(4):
        fore_out[d] = fore[d][...]
        if inner:
            for n in range(4):
                back_out[n, d] = back[d][n]
        else:
            back_out[d] = back[d][...]


def stack_lines(fore, back):
    out = like((4, *fore[0].shape), bf16)
    return call(functools.partial(stack_kernel, False), (*fore, *back), [out, out])


def stack_planes(fore, back):
    out = like((4, *fore[0].shape), bf16)
    return call(functools.partial(stack_kernel, True), (*fore, *back), [out, out])


def product(left, right, flip):
    return lax.dot_general(
        left, right, (((1,), (1 if flip else 0,)), ((), ())), preferred_element_type=f32
    )


def column_kernel(first, second, *outs):
    for rows, out in zip((first, second), outs):

        def add(i, total):
            return total + rows[pl.ds(pl.multiple_of(i * 16, 16), 16), :].astype(f32)

        total = lax.fori_loop(0, rows.shape[0] // 16, add, jnp.zeros((16, rows.shape[1]), f32), unroll=4)
        out[...] = jnp.sum(total, axis=0, keepdims=out.ndim == 2)


def column_sums(first, second):
    return call(column_kernel, (first, second), [like((v.shape[1],), f32) for v in (first, second)])


SENT, KEPT = (4, -3, 1), (0, 3, 2, -2, -1)


def into_hidden_kernel(turn, flip, place, own, other, weight, *outs):
    terms, rows, part = outs[:8], outs[8], outs[-1]
    step = part.shape[1]
    rows[0:384, :] = own[...]
    rows[384:768, :] = other[...]

    @pl.loop(0, terms[0].shape[1] // step)
    def _(j):
        here = pl.ds(pl.multiple_of(j * step, step), step)
        part[...] = product(rows[...], weight[here, :] if flip else weight[:, here], flip)
        for out, k in zip(terms, SENT + KEPT):
            first = pl.multiple_of(lax.rem(place[0] + turn * k + 16, 8) * 96, 96)
            out[:, here] = part[pl.ds(first, 96), :].astype(out.dtype)


def into_hidden(place, own, other, weight, turn, flip):
    k = own.shape[1]
    n = weight.shape[0] if flip else weight.shape[1]
    got = call(
        functools.partial(into_hidden_kernel, turn, flip),
        (place, own, other, weight),
        [like((96, n), bf16)] * 3 + [like((96, n), f32)] * 5 + [like((768, k), bf16)],
        flops=2 * 768 * n * k,
        scratch=[pltpu.VMEM((768, 256), f32)],
    )
    return dict(zip(SENT + KEPT, got[:8])), *got[8:]


def out_of_hidden_kernel(flip, place, *refs):
    blocks, weight, (keep, send, rows) = refs[:8], refs[8], refs[9:]
    for k in range(8):
        first = pl.multiple_of(lax.rem(place[0] + k, 8) * 96, 96)
        rows[pl.ds(first, 96), :] = blocks[k][...]
    step = 256

    @pl.loop(0, keep.shape[1] // step)
    def _(j):
        here = pl.ds(pl.multiple_of(j * step, step), step)
        part = product(rows[...], weight[here, :] if flip else weight[:, here], flip)
        keep[:, here] = part[:384]
        send[:, here] = part[384:].astype(bf16)


def out_of_hidden(place, blocks, weight, flip):
    k = blocks[0].shape[1]
    n = weight.shape[0] if flip else weight.shape[1]
    return call(
        functools.partial(out_of_hidden_kernel, flip),
        (place, *blocks, weight),
        [like((384, n), f32), like((384, n), bf16), like((768, k), bf16)],
        flops=2 * 768 * n * k,
    )


def chip_kernel(by_x, keep, got, *outs):
    for d in range(4):
        if by_x:
            total = keep[:, d] + got[:, d].astype(f32)
        else:
            total = keep[d] + got[d].astype(f32)
        outs[d][...] = total.astype(outs[d].dtype)


def chip_sums(keep, got, by_x):
    n = keep.shape[1]
    return call(
        functools.partial(chip_kernel, by_x),
        [v.reshape(4, 4, 24, n) for v in (keep, got)],
        [like((4, 24, n), f32)] + [like((4, 24, n), bf16)] * 3,
    )


def line_kernel(*refs):
    for ins, outs in ((refs[0:4], refs[8:12]), (refs[4:8], refs[12:16])):
        for d in range(4):
            total = ins[0][d]
            for v in ins[1:]:
                total += v[d].astype(f32)
            outs[d][...] = total.astype(outs[d].dtype)


def line_sums(fore, back):
    n = fore[0].shape[2]
    f_types, b_types = (f32, bf16, bf16, bf16), (f32, f32, bf16, f32)
    return call(line_kernel, (*fore, *back), [like((24, n), t) for t in f_types + b_types])


def gather_four(v, move, direct):
    one = move(v, -1)
    three = move(v, 1)
    two = move(v, 2) if direct else move(one, -1)
    return [v, one, two, three]


def gather_both(fore, back):
    width = fore.shape[1]
    fore, back = stack_lines(gather_four(fore, along_x, True), gather_four(back, along_y, True))
    fore, back = stack_planes(gather_four(fore, along_y, False), gather_four(back, along_x, False))
    return fore.reshape(384, width), back.reshape(384, width)


def collect_row(share, turn):
    blocks = {0: share}
    ahead = behind = share
    for k in (1, 2, 3, 4):
        ahead = along_z(ahead, turn)
        blocks[-turn * k % 8] = ahead
        if k < 4:
            behind = along_z(behind, -turn)
            blocks[turn * k % 8] = behind
    return [blocks[k] for k in range(8)]


def reduce_row(terms, turn):
    def sent(v, k):
        return along_z(v.astype(bf16), turn * k).astype(f32)

    up, down, near = sent(terms[4], 1), sent(terms[-3], -1), sent(terms[1], 1)
    up, down = sent(up + terms[3], 1), sent(down + terms[-2], -1)
    up, down = sent(up + terms[2], 2), sent(down + terms[-1], -1)
    return terms[0] + up + down + near


def scatter_four(pieces, move):
    return [pieces[0], move(pieces[2], 2), move(pieces[1], 1), move(pieces[3], -1)]


def contract_first(left, right):
    return lax.dot_general(left, right, (((0,), (0,)), ((), ())), preferred_element_type=f32)


def body(tokens, widen, offsets, narrow, shifts, cotangent):
    place = lax.axis_index("row").astype(jnp.int32).reshape(1)
    tok_own, cot_own = gather_both(tokens, cotangent)
    fore, tok_all = into_hidden(place, tok_own, swap_cores(tok_own), widen, 1, False)
    back, cot_all = into_hidden(place, cot_own, swap_cores(cot_own), narrow, -1, True)
    value, slope = gelu_parts(reduce_row(fore, 1) + offsets.astype(f32))
    act_grad = reduce_row(back, -1)
    act_blocks = collect_row(value.astype(bf16), 1)
    grad_blocks = collect_row((act_grad * slope).astype(bf16), -1)
    act_blocks, grad_blocks = lax.optimization_barrier((act_blocks, grad_blocks))
    f_keep, f_send, act_all = out_of_hidden(place, act_blocks, narrow, False)
    b_keep, b_send, grad_all = out_of_hidden(place, grad_blocks, widen, True)
    f_got, b_got = swap_cores(f_send), swap_cores(b_send)
    fore, back = chip_sums(f_keep, f_got, False), chip_sums(b_keep, b_got, True)
    grad_late, *pieces = lax.optimization_barrier((grad_all, *fore, *back))
    fore, back = scatter_four(pieces[:4], along_y), scatter_four(pieces[4:], along_x)
    grad_late, fore[1] = lax.optimization_barrier((grad_late, fore[1]))
    widen_grad = contract_first(tok_all, grad_late).astype(bf16)
    offsets_grad, shifts_grad = column_sums(grad_late, cot_all)
    widen_grad, offsets_grad, shifts_grad, fore, back = lax.optimization_barrier(
        (widen_grad, offsets_grad, shifts_grad, fore, back)
    )
    lines = line_sums(fore, back)
    fore, back = scatter_four(lines[:4], along_x), scatter_four(lines[4:], along_y)
    act_late, fore[1] = lax.optimization_barrier((act_all, fore[1]))
    narrow_grad = contract_first(act_late, cot_all).astype(bf16)
    layer_out = (sum(v.astype(f32) for v in fore) + shifts.astype(f32)).astype(bf16)
    token_grad = sum(v.astype(f32) for v in back).astype(bf16)
    return (layer_out, token_grad, widen_grad, narrow_grad, offsets_grad, shifts_grad)


def solution(mesh):
    return jax.shard_map(
        body,
        mesh=mesh,
        in_specs=(
            P(("col", "depth"), "row"),
            P("row", ("col", "depth")),
            P(("col", "depth")),
            P(("col", "depth"), "row"),
            P("row"),
            P(("col", "depth"), "row"),
        ),
        out_specs=(
            P(("col", "depth"), "row"),
            P(("col", "depth"), "row"),
            P("row", ("col", "depth")),
            P(("col", "depth"), "row"),
            P(("col", "depth")),
            P("row"),
        ),
        check_vma=False,
    )
```
